512 devices in a mesh: section: 32 (over z, core), seq: 16 (over x, y).
Axes of the slice: x: 4, y: 4, z: 16, core: 2. Of those that a mesh axis runs over, the one named last changes fastest.
Arguments:
- slices: bfloat16 [32, 2048, 1024], P('section', 'seq'), may hold values from -6 to 6
- new_slice: bfloat16 [2048, 1024], P('seq'), may hold values from -6 to 6
- w_qkv: bfloat16 [32, 1024, 3072], P('section', None, 'seq'), may hold values from -0.1875 to 0.1875
- w_gate: bfloat16 [32, 1024, 1024], P('section', None, 'seq'), may hold values from -0.1875 to 0.1875
- w_out: bfloat16 [32, 1024, 1024], P('section', 'seq'), may hold values from -0.1875 to 0.1875
- input_gain: float32 [32, 1024], P('section'), may hold values from 0.25 to 1.75
- output_gain: float32 [32, 1024], P('section'), may hold values from 0.25 to 1.75
- bucket_bias: bfloat16 [32, 16, 64], P('section'), may hold values from -6 to 6
- repeat_bias: float32 [32, 16], P('section'), may hold values from -6 to 6
- cache_kv: bfloat16 [32, 768, 16, 128], P('section', None, 'seq'), may hold values from -6 to 6
- slice_positions: int32 [32, 2, 2048], P('section'), may hold values from 0 to 2815
- slice_buckets: int32 [32, 2, 2048], P('section'), may hold values from 0 to 63
- slice_items: int32 [32, 2, 2048], P('section'), may hold values from 0 to 511
- cache_positions: int32 [32, 768], P('section'), may hold values from 0 to 2815
- cache_buckets: int32 [32, 768], P('section'), may hold values from 0 to 63
- cache_items: int32 [32, 768], P('section'), may hold values from 0 to 511
Outputs:
- section_out: bfloat16 [32, 2, 2048, 1024], P('section', None, 'seq')
The draws below stay inside these ranges and needn't reach their ends.
All inputs are finite; a program needn't handle non-finite values.
Results may differ from the reference program's by a relative error of at most 0.009.
Values may be sent and summed in bfloat16 or wider, within the bound.
No kernel may reach another device: no remote copies, remote signals or barrier semaphores. Data moves between devices by JAX's collectives and lax.ppermute only.
A program may use at most 64 MiB of HBM per device.

```python
import math
import jax
import jax.numpy as jnp
import numpy as np
from jax import lax

D = 1024
H = 16
DH = 64
NB = 64
ITEMS = 512
TICKS = 2
CACHE = 768
SLICE = 2048
NK = 2816
N_SECTION = 32


def touch_ends(values, own_key, least, top_value):
    spot = [jax.random.randint(jax.random.fold_in(own_key, axis), (), 0, length) for axis, length in enumerate(values.shape)]
    longest = values.shape.index(max(values.shape))
    beside = spot[:longest] + [(spot[longest] + 1) % values.shape[longest]] + spot[longest + 1:]
    return values.at[tuple(spot)].set(least).at[tuple(beside)].set(top_value)


def steps_of(stream_key, dims, split, low, largest):
    factor_of = 1.0
    for position, shards_of in split:
        steps = jax.random.uniform(jax.random.fold_in(jax.random.fold_in(stream_key, 6), position), (shards_of,), jnp.float32, low / len(split), largest / len(split))
        factor_of = factor_of * jnp.repeat(jnp.exp(steps), dims[position] // shards_of).reshape((-1,) + (1,) * (len(dims) - 1 - position))
    return factor_of


def cumulative_ranks(amount, lean):
    loads = [(1 << 20) // math.isqrt(rank ** lean) + 1 for rank in range(1, amount + 1)]
    spread = 1 + sum(loads) // (1 << 30)
    return np.cumsum(np.array([max(1, weight // spread) for weight in loads]))


def ranked(rng, dims, count, slope):
    table = cumulative_ranks(count, slope)
    lot = jax.random.randint(jax.random.fold_in(rng, 1), dims, 0, int(table[count - 1]))
    standing = jnp.searchsorted(jnp.asarray(table, jnp.int32), lot, side="right")
    return jax.random.permutation(jax.random.fold_in(rng, 2), count)[standing].astype(jnp.int32)


def gaussian(stream_key, shape, width, most, split=(), kind=jnp.bfloat16):
    factor_of = steps_of(stream_key, shape, split, -0.22, 0.18) if split else 1.0
    values = jax.random.normal(stream_key, shape, jnp.float32) * width * factor_of
    return jnp.minimum(jnp.maximum(values, -most), most).astype(kind)


def setup_inputs(seed: int = 0) -> dict:
    key_list = jax.random.split(jax.random.key(seed), 17)
    return {
        "slices": gaussian(key_list[0], (N_SECTION, SLICE, D), 1.0, 6.0, ((0, 32), (1, 16))),
        "new_slice": gaussian(key_list[1], (SLICE, D), 1.0, 6.0, ((0, 16),)),
        "w_qkv": gaussian(key_list[2], (N_SECTION, D, 3 * D), D ** -0.5, 0.1875, ((0, 32), (2, 16))),
        "w_gate": gaussian(key_list[3], (N_SECTION, D, D), D ** -0.5, 0.1875, ((0, 32), (2, 16))),
        "w_out": gaussian(key_list[4], (N_SECTION, D, D), D ** -0.5, 0.1875, ((0, 32), (1, 16))),
        "input_gain": jnp.clip(1.0 + 0.15 * jax.random.normal(key_list[5], (N_SECTION, D), jnp.float32), 0.25, 1.75),
        "output_gain": jnp.clip(1.0 + 0.15 * jax.random.normal(key_list[6], (N_SECTION, D), jnp.float32), 0.25, 1.75),
        "bucket_bias": gaussian(key_list[7], (N_SECTION, H, NB), 1.5, 6.0, ((0, 32),)),
        "repeat_bias": gaussian(key_list[8], (N_SECTION, H), 2.0, 6.0, ((0, 32),), jnp.float32),
        "cache_kv": gaussian(key_list[9], (N_SECTION, CACHE, H, 2 * DH), 1.0, 6.0, ((0, 32), (2, 16))),
        "slice_positions": touch_ends(jax.random.randint(key_list[10], (N_SECTION, TICKS, SLICE), 0, NK), jax.random.fold_in(key_list[10], 1), 0, NK - 1).astype(jnp.int32),
        "slice_buckets": touch_ends(jax.random.randint(key_list[11], (N_SECTION, TICKS, SLICE), 0, NB), jax.random.fold_in(key_list[11], 1), 0, NB - 1).astype(jnp.int32),
        "slice_items": touch_ends(ranked(key_list[12], (N_SECTION, TICKS, SLICE), ITEMS, 2), jax.random.fold_in(key_list[12], 3), 0, ITEMS - 1).astype(jnp.int32),
        "cache_positions": touch_ends(jax.random.randint(key_list[13], (N_SECTION, CACHE), 0, NK), jax.random.fold_in(key_list[13], 1), 0, NK - 1).astype(jnp.int32),
        "cache_buckets": touch_ends(jax.random.randint(key_list[14], (N_SECTION, CACHE), 0, NB), jax.random.fold_in(key_list[14], 1), 0, NB - 1).astype(jnp.int32),
        "cache_items": touch_ends(ranked(key_list[15], (N_SECTION, CACHE), ITEMS, 2), jax.random.fold_in(key_list[15], 3), 0, ITEMS - 1).astype(jnp.int32),
    }


EPSILON = 1e-05

def norm_rows(values, gain):
    row_mean = lax.optimization_barrier(jnp.mean(values, axis=-1, keepdims=True))
    variance = lax.optimization_barrier(jnp.mean(values * values, axis=-1, keepdims=True)) - row_mean * row_mean
    return (values - row_mean) * lax.rsqrt(variance + EPSILON) * gain

def layer(inputs):
    current, weight_qkv, weight_gate, weight_out, gain_in, gain_out, table, repeat, cached, positions, buckets, items, cache_pos, cache_bkt, cache_itm = inputs
    resident = current.astype(jnp.float32)
    normed = norm_rows(resident, gain_in).astype(jnp.bfloat16)
    qkv = jax.nn.silu(jnp.dot(normed, weight_qkv, preferred_element_type=jnp.float32)).astype(jnp.bfloat16)
    gate = jax.nn.silu(jnp.dot(normed, weight_gate, preferred_element_type=jnp.float32))
    qkv = qkv.reshape(SLICE, H, 3 * DH)
    queries = jnp.transpose(qkv[:, :, :DH], (1, 0, 2))
    keys = jnp.transpose(jnp.concatenate([cached[:, :, :DH], qkv[:, :, DH:2 * DH]], axis=0), (1, 0, 2))
    values = jnp.transpose(jnp.concatenate([cached[:, :, DH:], qkv[:, :, 2 * DH:]], axis=0), (1, 0, 2))
    key_pos = jnp.concatenate([cache_pos, positions])
    key_bkt = jnp.concatenate([cache_bkt, buckets])
    key_itm = jnp.concatenate([cache_itm, items])
    allowed = key_pos[None, :] <= positions[:, None]
    distance = jnp.abs(buckets[:, None] - key_bkt[None, :]).astype(jnp.int32)
    same_item = items[:, None] == key_itm[None, :]

    def head_attention(head_inputs):
        query, key, value, bias_row, rep = head_inputs
        scores = jnp.dot(query, key.T, preferred_element_type=jnp.float32)
        scores = scores + jnp.take(bias_row.astype(jnp.float32), distance) + jnp.where(same_item, rep, 0.0)
        weights = jnp.where(allowed, jax.nn.silu(scores) / NK, 0.0).astype(jnp.bfloat16)
        return jnp.dot(weights, value, preferred_element_type=jnp.float32).astype(jnp.bfloat16)
    attended = lax.map(head_attention, (queries, keys, values, table, repeat))
    attended = jnp.transpose(attended, (1, 0, 2)).reshape(SLICE, D)
    mixed = (norm_rows(attended.astype(jnp.float32), gain_out) * gate).astype(jnp.bfloat16)
    return (resident + jnp.dot(mixed, weight_out, preferred_element_type=jnp.float32)).astype(jnp.bfloat16)

def reference(slices, new_slice, w_qkv, w_gate, w_out, input_gain, output_gain, bucket_bias, repeat_bias, cache_kv, slice_positions, slice_buckets, slice_items, cache_positions, cache_buckets, cache_items):

    def run_tick(tick_index, section_inputs):
        return lax.map(layer, (section_inputs, w_qkv, w_gate, w_out, input_gain, output_gain, bucket_bias, repeat_bias, cache_kv, slice_positions[:, tick_index], slice_buckets[:, tick_index], slice_items[:, tick_index], cache_positions, cache_buckets, cache_items))
    outputs = []
    current = slices
    for tick_index in range(TICKS):
        produced = run_tick(tick_index, current)
        outputs.append(produced)
        current = jnp.concatenate([new_slice[None], produced[:-1]], axis=0)
    return jnp.stack(outputs, axis=1)
```

```python
import jax
import jax.numpy as jnp
from jax import lax
from jax.experimental import pallas as pl
from jax.experimental.pallas import tpu as pltpu
from jax.sharding import Mesh, PartitionSpec as P

D = 1024
H = 16
DH = 64
NB = 64
TICKS = 2
CACHE = 768
SLICE = 2048
NK = CACHE + SLICE
EPSILON = 1e-05
NP = 2
NG = 8
ROWS = SLICE // (NP * NG)
BAND = SLICE // NP
KBLOCK = 256
BF16 = jnp.bfloat16
F32 = jnp.float32
VMEM_LIMIT = 60 * 1024 * 1024


def silu(v):
    half = 0.5 * v
    return half + half * jnp.tanh(half)


def vmem():
    return pl.BlockSpec(memory_space=pltpu.VMEM)


def smem():
    return pl.BlockSpec(memory_space=pltpu.SMEM)


def params():
    return pltpu.CompilerParams(vmem_limit_bytes=VMEM_LIMIT)


def low_lanes(rows):
    return lax.broadcasted_iota(jnp.int32, (rows, 2 * DH), 1) < DH


def project_kernel(p_ref, x_ref, own_ref, other_ref, gain_ref, qb_ref, lhs_ref, kv_ref, gate_ref, first):
    p = p_ref[0]
    values = x_ref[...].reshape(BAND, D).astype(F32)
    mean = jnp.mean(values, axis=-1, keepdims=True)
    variance = jnp.mean(values * values, axis=-1, keepdims=True) - mean * mean
    normed = ((values - mean) * lax.rsqrt(variance + EPSILON) * gain_ref[...]).astype(BF16)
    low = low_lanes(BAND)
    for index, w_ref in ((p, own_ref), (1 - p, other_ref)):
        z = silu(jnp.dot(normed, w_ref[...], preferred_element_type=F32))
        kv_ref[index] = z[:, 2 * DH :].astype(BF16)
        first[index] = z[:, : 2 * DH]
    for h in range(NP):
        lhs_ref[h] = jnp.where(low, 0.5 * first[h], qb_ref[h].astype(F32)).astype(BF16)
    gate_ref[...] = jnp.where(low, pltpu.roll(first[0], DH, 1), first[1]).astype(BF16)


def project(p, x, own, other, gain, qb):
    return pl.pallas_call(
        project_kernel,
        out_shape=(
            jax.ShapeDtypeStruct((NP, BAND, 2 * DH), BF16),
            jax.ShapeDtypeStruct((NP, BAND, 2 * DH), BF16),
            jax.ShapeDtypeStruct((BAND, 2 * DH), BF16),
        ),
        in_specs=[smem()] + [vmem()] * 5,
        out_specs=(vmem(), vmem(), vmem()),
        scratch_shapes=[pltpu.VMEM((NP, BAND, 2 * DH), F32)],
        compiler_params=params(),
        name="project",
    )(p, x, own, other, gain, qb)


def add_keys(rep_ref, lhs_ref, qpos_ref, qitm_ref, same, allowed, acc, kv_ref, ko_ref, kpos_ref, kitm_ref, fresh):
    count = kv_ref.shape[1]
    low = low_lanes(KBLOCK)
    for c in range(count // KBLOCK):
        ks = slice(c * KBLOCK, (c + 1) * KBLOCK)
        same[...] = jnp.where(qitm_ref[...] == kitm_ref[:, ks], 1.0, 0.0)
        allowed[...] = jnp.where(kpos_ref[:, ks] <= qpos_ref[...], 1.0, 0.0).astype(BF16)
        for h in range(NP):
            kv = kv_ref[h, ks, :]
            keys = jnp.where(low, kv, ko_ref[ks, :])
            half = lax.dot_general(lhs_ref[h], keys, (((1,), (1,)), ((), ())), preferred_element_type=F32)
            half = half + (0.5 * rep_ref[h]) * same[...]
            weight = (half + half * jnp.tanh(half)).astype(BF16) * allowed[...]
            part = jnp.dot(weight, kv, preferred_element_type=F32)
            if fresh and c == 0:
                acc[h] = part
            else:
                acc[h] += part


def early_kernel(rep_ref, lhs_ref, qpos_ref, qitm_ref, ckv_ref, cko_ref, cpos_ref, citm_ref, kv_ref, ko_ref, kpos_ref, kitm_ref, acc, same, allowed):
    shared = (rep_ref, lhs_ref, qpos_ref, qitm_ref, same, allowed, acc)
    add_keys(*shared, kv_ref, ko_ref, kpos_ref, kitm_ref, True)
    add_keys(*shared, ckv_ref, cko_ref, cpos_ref, citm_ref, False)


def late_kernel(rep_ref, lhs_ref, qpos_ref, qitm_ref, acc_ref, kv_ref, ko_ref, kpos_ref, kitm_ref, out_ref, acc, same, allowed):
    acc[...] = acc_ref[...]
    add_keys(rep_ref, lhs_ref, qpos_ref, qitm_ref, same, allowed, acc, kv_ref, ko_ref, kpos_ref, kitm_ref, False)
    out_ref[...] = (jnp.where(low_lanes(BAND), pltpu.roll(acc[0], DH, 1), acc[1]) * (1.0 / NK)).astype(BF16)


MASKS = [pltpu.VMEM((BAND, KBLOCK), F32), pltpu.VMEM((BAND, KBLOCK), BF16)]


def attend_early(*operands):
    return pl.pallas_call(
        early_kernel,
        out_shape=jax.ShapeDtypeStruct((NP, BAND, 2 * DH), F32),
        in_specs=[smem()] + [vmem()] * 11,
        out_specs=vmem(),
        scratch_shapes=MASKS,
        compiler_params=params(),
        name="attend_early",
    )(*operands)


def attend_late(*operands):
    return pl.pallas_call(
        late_kernel,
        out_shape=jax.ShapeDtypeStruct((BAND, 2 * DH), BF16),
        in_specs=[smem()] + [vmem()] * 8,
        out_specs=vmem(),
        scratch_shapes=[pltpu.VMEM((NP, BAND, 2 * DH), F32)] + MASKS,
        compiler_params=params(),
        name="attend_late",
    )(*operands)


def finish_kernel(r_ref, g_ref, x_ref, w_ref, gain_ref, out_ref, mixed):
    total = jnp.zeros((ROWS, 2 * DH), F32)
    square = jnp.zeros((ROWS, 2 * DH), F32)
    for k in range(NG):
        a = r_ref[k].astype(F32)
        total += a
        square += a * a
    mean = jnp.sum(total, axis=-1, keepdims=True) * (1.0 / D)
    variance = jnp.sum(square, axis=-1, keepdims=True) * (1.0 / D) - mean * mean
    scale = lax.rsqrt(variance + EPSILON)
    for k in range(NG):
        cols = slice(k * 2 * DH, (k + 1) * 2 * DH)
        a = r_ref[k].astype(F32)
        mixed[:, cols] = ((a - mean) * scale * gain_ref[:, cols] * g_ref[k].astype(F32)).astype(BF16)
    y = jnp.dot(mixed[...], w_ref[...], preferred_element_type=F32)
    out_ref[...] = (x_ref[...].astype(F32) + y).astype(BF16)


def finish(*operands):
    return pl.pallas_call(
        finish_kernel,
        out_shape=jax.ShapeDtypeStruct((ROWS, D), BF16),
        in_specs=[vmem()] * 5,
        out_specs=vmem(),
        scratch_shapes=[pltpu.VMEM((ROWS, D), BF16)],
        compiler_params=params(),
        name="finish",
    )(*operands)


def gather_g(x):
    return lax.all_to_all(jnp.broadcast_to(x[None], (NG,) + x.shape), "g", 0, 0)


def swap(x):
    return lax.ppermute(x, "p", [(0, 1), (1, 0)])


def body(
    slices,
    new_slice,
    w_qkv,
    w_gate,
    w_out,
    input_gain,
    output_gain,
    bucket_bias,
    repeat_bias,
    cache_kv,
    slice_positions,
    slice_buckets,
    slice_items,
    cache_positions,
    cache_buckets,
    cache_items,
):
    p = lax.axis_index("p")
    g = lax.axis_index("g")
    section = lax.axis_index("section")

    def both(own):
        other = swap(own)
        return jnp.stack([jnp.where(p == 0, own, other), jnp.where(p == 0, other, own)])

    w_own = jnp.concatenate([w_qkv[0, :, :DH], w_gate[0], w_qkv[0, :, DH:]], axis=1)
    w_other = swap(w_own)
    cached = both(cache_kv[0, :, 0, :])
    w_out_full = gather_g(both(w_out[0])).reshape(D, D)
    gain_out = output_gain[0].reshape(NP, NG, DH).transpose(1, 0, 2).reshape(1, D)
    tables = lax.dynamic_slice_in_dim(bucket_bias[0].reshape(NP, NG, NB), g, 1, 1)[:, 0]
    rep = lax.dynamic_slice_in_dim(repeat_bias[0].reshape(NP, NG), g, 1, 1)[:, 0]
    levels = jnp.arange(NB, dtype=jnp.int32)
    distance = jnp.abs(levels[:, None] - levels[None, :])
    lookup = (distance[:, :, None] == levels[None, None, :]).astype(F32)
    toeplitz = jnp.einsum("abc,hc->hab", lookup, tables.astype(F32)).astype(BF16)
    toeplitz = jnp.pad(0.5 * toeplitz, ((0, 0), (0, 0), (DH, 0)))
    lanes = jnp.arange(2 * DH, dtype=jnp.int32) - DH

    def key_side(bkt, pos, itm):
        return (bkt[:, None] == lanes[None, :]).astype(BF16), pos[None, :], itm[None, :]

    cache_side = key_side(cache_buckets[0], cache_positions[0], cache_items[0])
    p_word = p.astype(jnp.int32).reshape(1)

    current = slices[0]
    outputs = []
    for tick in range(TICKS):
        positions = slice_positions[0, tick].reshape(NP, BAND)
        buckets = slice_buckets[0, tick].reshape(NP, BAND)
        items = slice_items[0, tick].reshape(NP, BAND)

        def take(a, i):
            return lax.dynamic_index_in_dim(a, i, 0, keepdims=False)

        own_side = key_side(take(buckets, p), take(positions, p), take(items, p))
        other_side = key_side(take(buckets, 1 - p), take(positions, 1 - p), take(items, 1 - p))
        qpos = take(positions, p)[:, None]
        qitm = take(items, p)[:, None]
        query_onehot = (take(buckets, p)[:, None] == levels[None, :]).astype(BF16)
        query_bias = jnp.einsum("sa,hab->hsb", query_onehot, toeplitz, preferred_element_type=F32).astype(BF16)
        band = gather_g(current)
        lhs, kv, gate = project(p_word, band, w_own, w_other, input_gain, query_bias)
        kv_other = swap(kv)
        gates = lax.all_to_all(gate.reshape(NG, ROWS, 2 * DH), "g", 0, 0)
        acc = attend_early(rep, lhs, qpos, qitm, cached, *cache_side, kv, *own_side)
        a = attend_late(rep, lhs, qpos, qitm, acc, kv_other, *other_side)
        back = lax.all_to_all(a.reshape(NG, ROWS, 2 * DH), "g", 0, 0)
        produced = finish(back, gates, current, w_out_full, gain_out)
        outputs.append(produced)
        if tick + 1 < TICKS:
            count = lax.axis_size("section")
            shifted = lax.ppermute(produced, "section", [(s, s + 1) for s in range(count - 1)])
            current = jnp.where(section == 0, new_slice, shifted)
    return jnp.stack(outputs, axis=0)[None]


def solution(mesh):
    sections = mesh.shape["section"]
    grid = Mesh(mesh.devices.reshape(sections, NP, NG), ("section", "p", "g"))
    seq = ("p", "g")
    in_specs = (
        P("section", seq, None),
        P(seq, None),
        P("section", None, seq),
        P("section", None, seq),
        P("section", seq, None),
        P("section", None),
        P("section", None),
        P("section", None, None),
        P("section", None),
        P("section", None, seq, None),
        P("section", None, None),
        P("section", None, None),
        P("section", None, None),
        P("section", None),
        P("section", None),
        P("section", None),
    )
    out_specs = P("section", None, seq, None)
    return jax.shard_map(body, mesh=grid, in_specs=in_specs, out_specs=out_specs, check_vma=False)
```

```python
import functools

import jax
import jax.numpy as jnp
from jax import lax
from jax.experimental import pallas as pl
from jax.experimental.pallas import tpu as pltpu
from jax.sharding import Mesh, PartitionSpec as P

D = 1024
H = 16
DH = 64
NB = 64
TICKS = 2
CACHE = 768
SLICE = 2048
NK = CACHE + SLICE
EPSILON = 1e-05
NP = 2
NG = 8
ROWS = SLICE // (NP * NG)
BAND = SLICE // NP
KBLOCK = 256
PART = ROWS // 2
HALF = BAND // 2
BF16 = jnp.bfloat16
F32 = jnp.float32
VMEM_LIMIT = 60 * 1024 * 1024


def silu(v):
    half = 0.5 * v
    return half + half * jnp.tanh(half)


def vmem():
    return pl.BlockSpec(memory_space=pltpu.VMEM)


def smem():
    return pl.BlockSpec(memory_space=pltpu.SMEM)


def params():
    return pltpu.CompilerParams(vmem_limit_bytes=VMEM_LIMIT)


def low_lanes(rows):
    return lax.broadcasted_iota(jnp.int32, (rows, 2 * DH), 1) < DH


def spread_kernel(first_ref, x_ref, new_ref, gain_ref, here_ref, one_ref, two_ref):
    fresh = jnp.full((ROWS, 1), first_ref[0], jnp.int32) > 0
    here = jnp.where(fresh, new_ref[...].astype(F32), x_ref[...].astype(F32))
    here_ref[...] = here.astype(BF16)
    mean = jnp.mean(here, axis=-1, keepdims=True)
    variance = jnp.mean(here * here, axis=-1, keepdims=True) - mean * mean
    normed = ((here - mean) * lax.rsqrt(variance + EPSILON) * gain_ref[...]).astype(BF16)
    for k in range(NG):
        one_ref[k] = normed[:PART]
        two_ref[k] = normed[PART:]


def spread(*operands):
    return pl.pallas_call(
        spread_kernel,
        out_shape=(jax.ShapeDtypeStruct((ROWS, D), BF16),) + (jax.ShapeDtypeStruct((NG, PART, D), BF16),) * 2,
        in_specs=[smem()] + [vmem()] * 3,
        out_specs=(vmem(),) * 3,
        compiler_params=params(),
        name="spread",
    )(*operands)


def column(row):
    return jnp.transpose(jnp.broadcast_to(row, (128, row.shape[1])))


def prep_kernel(tick, p_ref, meta_ref, cbkt_ref, table_ref, qpos_ref, qitm_ref, qb_ref, ko_ref, cko_ref, krow_ref):
    lane = lax.broadcasted_iota(jnp.int32, (BAND, 128), 1)
    flip = jnp.full((1, BAND), p_ref[0], jnp.int32) > 0

    def bands(k):
        row = meta_ref[k * TICKS + tick : k * TICKS + tick + 1, :]
        low, high = row[:, :BAND], row[:, BAND:]
        return jnp.where(flip, high, low), jnp.where(flip, low, high)

    pos, bkt, itm = bands(0), bands(1), bands(2)
    qpos_ref[...] = column(pos[0])
    qitm_ref[...] = column(itm[0])
    for b in range(NP):
        level = column(bkt[b])
        ko_ref[b] = jnp.where(level == lane - DH, 1.0, 0.0).astype(BF16)
        krow_ref[b, 0:1, :] = pos[b]
        krow_ref[b, 1:2, :] = itm[b]
        if b == 0:
            onehot = jnp.where(level == lane, 1.0, 0.0).astype(BF16)
            for h in range(NP):
                qb_ref[h] = jnp.dot(onehot, table_ref[h], preferred_element_type=F32).astype(BF16)
    cko_ref[...] = jnp.where(column(cbkt_ref[...]) == lane[:CACHE] - DH, 1.0, 0.0).astype(BF16)


def prep(tick, *operands):
    return pl.pallas_call(
        functools.partial(prep_kernel, tick),
        out_shape=(
            jax.ShapeDtypeStruct((BAND, 128), jnp.int32),
            jax.ShapeDtypeStruct((BAND, 128), jnp.int32),
            jax.ShapeDtypeStruct((NP, BAND, 128), BF16),
            jax.ShapeDtypeStruct((NP, BAND, 128), BF16),
            jax.ShapeDtypeStruct((CACHE, 128), BF16),
            jax.ShapeDtypeStruct((NP, 2, BAND), jnp.int32),
        ),
        in_specs=[smem()] + [vmem()] * 3,
        out_specs=(vmem(),) * 6,
        compiler_params=params(),
        name="prep",
    )(*operands)


def project_kernel(half, p_ref, x_ref, own_ref, other_ref, qb_ref, lhs_ref, kv_ref, gate_ref):
    normed = x_ref[...].reshape(HALF, D)
    low = low_lanes(HALF)
    rows = slice(half * HALF, (half + 1) * HALF)
    firsts = []
    for h, w_ref in enumerate((own_ref, other_ref)):
        z = silu(jnp.dot(normed, w_ref[...], preferred_element_type=F32))
        kv_ref[h] = z[:, 2 * DH :].astype(BF16)
        first = z[:, : 2 * DH]
        lhs_ref[h] = jnp.where(low, 0.5 * first, qb_ref[h, rows, :].astype(F32)).astype(BF16)
        firsts.append(first)
    flip = jnp.full((HALF, 1), p_ref[0], jnp.int32) > 0
    left = jnp.where(flip, firsts[1], firsts[0])
    right = jnp.where(flip, firsts[0], firsts[1])
    gate_ref[...] = jnp.where(low, pltpu.roll(left, DH, 1), right).astype(BF16)


def project(half, *operands):
    return pl.pallas_call(
        functools.partial(project_kernel, half),
        out_shape=(
            jax.ShapeDtypeStruct((NP, HALF, 2 * DH), BF16),
            jax.ShapeDtypeStruct((NP, HALF, 2 * DH), BF16),
            jax.ShapeDtypeStruct((HALF, 2 * DH), BF16),
        ),
        in_specs=[smem()] + [vmem()] * 4,
        out_specs=(vmem(),) * 3,
        compiler_params=params(),
        name="project",
    )(*operands)


def add_keys(rep_ref, lhs_ref, qpos_ref, qitm_ref, same, allowed, acc, rows, kv_refs, ko, kpos, kitm, fresh):
    count = kv_refs[0].shape[0]
    size = rows.stop - rows.start
    low = low_lanes(KBLOCK)
    for c in range(count // KBLOCK):
        ks = slice(c * KBLOCK, (c + 1) * KBLOCK)
        wide = jnp.concatenate([qitm_ref[rows, :]] * (KBLOCK // 128), axis=1)
        same[:size] = jnp.where(wide == kitm(ks), 1.0, 0.0)
        wide = jnp.concatenate([qpos_ref[rows, :]] * (KBLOCK // 128), axis=1)
        allowed[:size] = jnp.where(kpos(ks) <= wide, 1.0, 0.0).astype(BF16)
        for h in range(NP):
            kv = kv_refs[h][ks, :]
            keys = jnp.where(low, kv, ko(ks))
            half = lax.dot_general(lhs_ref[h, rows, :], keys, (((1,), (1,)), ((), ())), preferred_element_type=F32)
            half = half + (0.5 * rep_ref[h]) * same[:size]
            weight = (half + half * jnp.tanh(half)).astype(BF16) * allowed[:size]
            part = jnp.dot(weight, kv, preferred_element_type=F32)
            if fresh and c == 0:
                acc[h, rows, :] = part
            else:
                acc[h, rows, :] += part


FIRST, SECOND, WHOLE = slice(0, HALF), slice(HALF, BAND), slice(0, BAND)


def sides(ko_ref, krow_ref, band, half):
    base = half * HALF

    def at(ks):
        return slice(base + ks.start, base + ks.stop)

    return (
        lambda ks: ko_ref[band, at(ks), :],
        lambda ks: krow_ref[band, 0:1, at(ks)],
        lambda ks: krow_ref[band, 1:2, at(ks)],
    )


def cache_sides(cko_ref, crow_ref):
    return (lambda ks: cko_ref[ks, :], lambda ks: crow_ref[0:1, ks], lambda ks: crow_ref[1:2, ks])


def one_kernel(rep_ref, qpos_ref, qitm_ref, ko_ref, krow_ref, cko_ref, crow_ref, cown_ref, cother_ref, lhs_ref, kv_ref, acc, same, allowed):
    shared = (rep_ref, lhs_ref, qpos_ref, qitm_ref, same, allowed, acc, FIRST)
    add_keys(*shared, (cown_ref, cother_ref), *cache_sides(cko_ref, crow_ref), True)
    add_keys(*shared, (kv_ref.at[0], kv_ref.at[1]), *sides(ko_ref, krow_ref, 0, 0), False)


def two_kernel(rep_ref, qpos_ref, qitm_ref, ko_ref, krow_ref, cko_ref, crow_ref, cown_ref, cother_ref, lhs1_ref, kv1_ref, acc1_ref, lhs2_ref, kv2_ref, far1_ref, acc, lhs, same, allowed):
    for h in range(NP):
        lhs[h, FIRST, :] = lhs1_ref[h]
        lhs[h, SECOND, :] = lhs2_ref[h]
        acc[h, FIRST, :] = acc1_ref[h]
    shared = (rep_ref, lhs, qpos_ref, qitm_ref, same, allowed, acc)
    add_keys(*shared, SECOND, (cown_ref, cother_ref), *cache_sides(cko_ref, crow_ref), True)
    add_keys(*shared, SECOND, (kv1_ref.at[0], kv1_ref.at[1]), *sides(ko_ref, krow_ref, 0, 0), False)
    add_keys(*shared, WHOLE, (kv2_ref.at[0], kv2_ref.at[1]), *sides(ko_ref, krow_ref, 0, 1), False)
    add_keys(*shared, WHOLE, (far1_ref.at[1], far1_ref.at[0]), *sides(ko_ref, krow_ref, 1, 0), False)


def three_kernel(rep_ref, p_ref, qpos_ref, qitm_ref, ko_ref, krow_ref, lhs1_ref, lhs2_ref, acc_ref, gate1_ref, gate2_ref, far2_ref, out_ref, acc, lhs, same, allowed):
    for h in range(NP):
        lhs[h, FIRST, :] = lhs1_ref[h]
        lhs[h, SECOND, :] = lhs2_ref[h]
    acc[...] = acc_ref[...]
    add_keys(rep_ref, lhs, qpos_ref, qitm_ref, same, allowed, acc, WHOLE, (far2_ref.at[1], far2_ref.at[0]), *sides(ko_ref, krow_ref, 1, 1), False)
    attended = (jnp.where(low_lanes(BAND), pltpu.roll(acc[p_ref[0]], DH, 1), acc[1 - p_ref[0]]) * (1.0 / NK)).astype(BF16)
    for half, gate_ref in enumerate((gate1_ref, gate2_ref)):
        for k in range(NG):
            rows = slice(half * PART, (half + 1) * PART)
            start = half * HALF + k * PART
            out_ref[k, rows, : 2 * DH] = attended[start : start + PART]
            out_ref[k, rows, 2 * DH :] = gate_ref[k * PART : (k + 1) * PART, :]


def masks(rows):
    return [pltpu.VMEM((rows, KBLOCK), F32), pltpu.VMEM((rows, KBLOCK), BF16)]


ACC = pltpu.VMEM((NP, BAND, 2 * DH), F32)
LHS = pltpu.VMEM((NP, BAND, 2 * DH), BF16)


def attend(kernel, shape, dtype, scratch, *operands):
    return pl.pallas_call(
        kernel,
        out_shape=jax.ShapeDtypeStruct(shape, dtype),
        in_specs=[smem() if a.ndim == 1 else vmem() for a in operands],
        out_specs=vmem(),
        scratch_shapes=scratch,
        compiler_params=params(),
        name="attend_" + kernel.__name__,
    )(*operands)


def finish_rows(r_ref, x_ref, w_ref, gain_ref, mixed):
    total = jnp.zeros((ROWS, 2 * DH), F32)
    square = jnp.zeros((ROWS, 2 * DH), F32)
    for k in range(NG):
        a = r_ref[k, :, : 2 * DH].astype(F32)
        total += a
        square += a * a
    mean = jnp.sum(total, axis=-1, keepdims=True) * (1.0 / D)
    variance = jnp.sum(square, axis=-1, keepdims=True) * (1.0 / D) - mean * mean
    scale = lax.rsqrt(variance + EPSILON)
    low = low_lanes(ROWS)
    for k in range(0, NG, 2):
        parts = []
        for r in (r_ref[k], r_ref[k + 1]):
            r = r.astype(F32)
            parts.append((r[:, : 2 * DH] - mean) * scale * r[:, 2 * DH :])
        left = jnp.where(low, parts[0], pltpu.roll(parts[1], DH, 1))
        right = jnp.where(low, pltpu.roll(parts[0], DH, 1), parts[1])
        for start, part in ((k * DH, left), (k * DH + D // 2, right)):
            cols = slice(start, start + 2 * DH)
            mixed[:, cols] = (part * gain_ref[:, cols]).astype(BF16)
    y = jnp.dot(mixed[...], w_ref[...], preferred_element_type=F32)
    return (x_ref[...].astype(F32) + y).astype(BF16)


def finish_kernel(r_ref, x_ref, w_ref, gain_ref, out_ref, mixed):
    out_ref[...] = finish_rows(r_ref, x_ref, w_ref, gain_ref, mixed)


def last_kernel(before_ref, r_ref, x_ref, w_ref, gain_ref, out_ref, mixed):
    out_ref[0] = before_ref[...]
    out_ref[1] = finish_rows(r_ref, x_ref, w_ref, gain_ref, mixed)


def finish(*operands):
    last = len(operands) == 5
    return pl.pallas_call(
        last_kernel if last else finish_kernel,
        out_shape=jax.ShapeDtypeStruct((TICKS, ROWS, D) if last else (ROWS, D), BF16),
        in_specs=[vmem()] * len(operands),
        out_specs=vmem(),
        scratch_shapes=[pltpu.VMEM((ROWS, D), BF16)],
        compiler_params=params(),
        name="finish_last" if last else "finish",
    )(*operands)


def swap(x):
    return lax.ppermute(x, "p", [(0, 1), (1, 0)])


def body(
    slices,
    new_slice,
    w_qkv,
    w_gate,
    w_out,
    input_gain,
    output_gain,
    bucket_bias,
    repeat_bias,
    cache_kv,
    slice_positions,
    slice_buckets,
    slice_items,
    cache_positions,
    cache_buckets,
    cache_items,
):
    p = lax.axis_index("p")
    g = lax.axis_index("g")
    section = lax.axis_index("section")

    w_out_full = lax.all_gather(w_out[0], ("p", "g"), axis=0, tiled=True)
    w_own = jnp.concatenate([w_qkv[0, :, :DH], w_gate[0], w_qkv[0, :, DH:]], axis=1)
    w_other = swap(w_own)
    c_own = cache_kv[0, :, 0, :]
    c_other = swap(c_own)

    def pair(a):
        a = a.reshape((NP, NG) + a.shape[1:])
        a = lax.dynamic_index_in_dim(a, g, 1, keepdims=False)
        return jnp.where(p == 0, a, a[::-1])

    tables = pair(bucket_bias[0])
    rep = pair(repeat_bias[0])
    levels = jnp.arange(NB, dtype=jnp.int32)
    distance = jnp.abs(levels[:, None] - levels[None, :])
    lookup = (distance[:, :, None] == levels[None, None, :]).astype(F32)
    toeplitz = jnp.einsum("abc,hc->hab", lookup, tables.astype(F32)).astype(BF16)
    toeplitz = jnp.pad(0.5 * toeplitz, ((0, 0), (0, DH), (DH, 0)))
    p_word = p.astype(jnp.int32).reshape(1)
    meta = jnp.stack([slice_positions[0], slice_buckets[0], slice_items[0]])
    meta = meta.reshape(3, TICKS, NP, NG, 2, PART).transpose(0, 1, 2, 4, 3, 5).reshape(3 * TICKS, SLICE)
    crow = jnp.concatenate([cache_positions, cache_items])
    preps = [prep(tick, p_word, meta, cache_buckets, toeplitz) for tick in range(TICKS)]

    received = slices[0]
    first = jnp.zeros((1,), jnp.int32)
    produced = ()
    for tick in range(TICKS):
        current, copies1, copies2 = spread(first, received, new_slice, input_gain)
        band1 = lax.all_to_all(copies1, "g", 0, 0)
        if tick == 0:
            band1, preps, crow, rep, w_own, w_other, c_other = lax.optimization_barrier(
                (band1, preps, crow, rep, w_own, w_other, c_other)
            )
        qpos, qitm, qb, ko, cko, krow = preps[tick]
        keyed = (rep, qpos, qitm, ko, krow)
        cache = (cko, crow, c_own, c_other)
        copies2, band1 = lax.optimization_barrier((copies2, band1))
        band2 = lax.all_to_all(copies2, "g", 0, 0)
        lhs1, kv1, gate1 = project(0, p_word, band1, w_own, w_other, qb)
        far1 = swap(kv1)
        acc1 = attend(one_kernel, (NP, HALF, 2 * DH), F32, masks(HALF), *keyed, *cache, lhs1, kv1)
        band2, acc1 = lax.optimization_barrier((band2, acc1))
        lhs2, kv2, gate2 = project(1, p_word, band2, w_own, w_other, qb)
        far2 = swap(kv2)
        acc = attend(two_kernel, (NP, BAND, 2 * DH), F32, [LHS] + masks(BAND), *keyed, *cache, lhs1, kv1, acc1, lhs2, kv2, far1)
        a = attend(three_kernel, (NG, ROWS, 4 * DH), BF16, [ACC, LHS] + masks(BAND), rep, p_word, *keyed[1:], lhs1, lhs2, acc, gate1, gate2, far2)
        back = lax.all_to_all(a, "g", 0, 0)
        if tick + 1 < TICKS:
            one = finish(back, current, w_out_full, output_gain)
            produced = (one,)
            count = lax.axis_size("section")
            received = lax.ppermute(one, "section", [(s, s + 1) for s in range(count - 1)])
            first = (section == 0).astype(jnp.int32).reshape(1)
    return finish(*produced, back, current, w_out_full, output_gain)[None]


def solution(mesh):
    sections = mesh.shape["section"]
    grid = Mesh(mesh.devices.reshape(sections, NP, NG), ("section", "p", "g"))
    seq = ("p", "g")
    in_specs = (
        P("section", seq, None),
        P(seq, None),
        P("section", None, seq),
        P("section", None, seq),
        P("section", seq, None),
        P("section", None),
        P("section", None),
        P("section", None, None),
        P("section", None),
        P("section", None, seq, None),
        P("section", None, None),
        P("section", None, None),
        P("section", None, None),
        P("section", None),
        P("section", None),
        P("section", None),
    )
    out_specs = P("section", None, seq, None)
    return jax.shard_map(body, mesh=grid, in_specs=in_specs, out_specs=out_specs, check_vma=False)
```

```python
import functools

import jax
import jax.numpy as jnp
from jax import lax
from jax.experimental import pallas as pl
from jax.experimental.pallas import tpu as pltpu
from jax.sharding import Mesh, PartitionSpec as P

D = 1024
H = 16
DH = 64
NB = 64
TICKS = 2
CACHE = 768
SLICE = 2048
NK = CACHE + SLICE
EPSILON = 1e-05
NP = 2
NG = 8
ROWS = SLICE // (NP * NG)
BAND = SLICE // NP
KBLOCK = 256
BF16 = jnp.bfloat16
F32 = jnp.float32
VMEM_LIMIT = 24 * 1024 * 1024


def silu(v):
    half = 0.5 * v
    return half + half * jnp.tanh(half)


def vmem():
    return pl.BlockSpec(memory_space=pltpu.VMEM)


def smem():
    return pl.BlockSpec(memory_space=pltpu.SMEM)


def params():
    return pltpu.CompilerParams(vmem_limit_bytes=VMEM_LIMIT)


def low_lanes(rows):
    return lax.broadcasted_iota(jnp.int32, (rows, 2 * DH), 1) < DH


def spread_kernel(first_ref, x_ref, new_ref, gain_ref, here_ref, out_ref):
    fresh = jnp.full((ROWS, 1), first_ref[0], jnp.int32) > 0
    here = jnp.where(fresh, new_ref[...].astype(F32), x_ref[...].astype(F32))
    here_ref[...] = here.astype(BF16)
    mean = jnp.mean(here, axis=-1, keepdims=True)
    variance = jnp.mean(here * here, axis=-1, keepdims=True) - mean * mean
    normed = ((here - mean) * lax.rsqrt(variance + EPSILON) * gain_ref[...]).astype(BF16)
    for k in range(NG):
        out_ref[k] = normed


def spread(*operands):
    return pl.pallas_call(
        spread_kernel,
        out_shape=(jax.ShapeDtypeStruct((ROWS, D), BF16), jax.ShapeDtypeStruct((NG, ROWS, D), BF16)),
        in_specs=[smem()] + [vmem()] * 3,
        out_specs=(vmem(),) * 2,
        compiler_params=params(),
        name="spread",
    )(*operands)


def column(row):
    return jnp.transpose(jnp.broadcast_to(row, (128, row.shape[1])))


def prepare(tick, p_ref, pos_ref, bkt_ref, itm_ref, table_ref, qg_ref, cbkt_ref, far, qpos, qitm, lhs, ko, krow, cko):
    lane = lax.broadcasted_iota(jnp.int32, (BAND, 128), 1)
    flip = jnp.full((1, BAND), p_ref[0], jnp.int32) > 0

    def bands(ref):
        low, high = ref[tick : tick + 1, :BAND], ref[tick : tick + 1, BAND:]
        return jnp.where(flip, high, low), jnp.where(flip, low, high)

    pos, bkt, itm = bands(pos_ref), bands(bkt_ref), bands(itm_ref)
    qpos[...] = column(pos[0])
    qitm[...] = column(itm[0])
    krow[0:1, :] = pos[far]
    krow[1:2, :] = itm[far]
    level = column(bkt[0])
    onehot = jnp.where(level == lane, 1.0, 0.0).astype(BF16)
    for h in range(NP):
        bias = jnp.dot(onehot, table_ref[h], preferred_element_type=F32)
        lhs[h] = jnp.where(lane < DH, qg_ref[h].astype(F32), bias).astype(BF16)
    level = column(bkt[1]) if far else level
    ko[...] = jnp.where(level == lane - DH, 1.0, 0.0).astype(BF16)
    if not far:
        cko[...] = jnp.where(column(cbkt_ref[...]) == lane[:CACHE] - DH, 1.0, 0.0).astype(BF16)


def project_kernel(x_ref, own_ref, other_ref, qg_ref, kv_ref, token_ref):
    token_ref[...] = jnp.zeros((8, 128), F32)
    normed = x_ref[...].reshape(BAND, D)
    scale = jnp.where(low_lanes(BAND), 0.5, 1.0)
    for h, w_ref in enumerate((own_ref, other_ref)):
        z = silu(jnp.dot(normed, w_ref[...], preferred_element_type=F32))
        kv_ref[h] = z[:, 2 * DH :].astype(BF16)
        qg_ref[h] = (z[:, : 2 * DH] * scale).astype(BF16)


def project(*operands):
    return pl.pallas_call(
        project_kernel,
        out_shape=(
            jax.ShapeDtypeStruct((NP, BAND, 2 * DH), BF16),
            jax.ShapeDtypeStruct((NP, BAND, 2 * DH), BF16),
            jax.ShapeDtypeStruct((8, 128), F32),
        ),
        in_specs=[vmem()] * 3,
        out_specs=(vmem(),) * 3,
        compiler_params=params(),
        name="project",
    )(*operands)


def add_keys(rep_ref, lhs_ref, qpos_ref, qitm_ref, same, allowed, acc, kv_refs, ko_ref, kpos_ref, kitm_ref, start):
    low = low_lanes(KBLOCK)
    for c in range(kv_refs[0].shape[0] // KBLOCK):
        ks = slice(c * KBLOCK, (c + 1) * KBLOCK)
        wide = jnp.concatenate([qitm_ref[...]] * (KBLOCK // 128), axis=1)
        same[...] = jnp.where(wide == kitm_ref[:, ks], 1.0, 0.0)
        wide = jnp.concatenate([qpos_ref[...]] * (KBLOCK // 128), axis=1)
        allowed[...] = jnp.where(kpos_ref[:, ks] <= wide, 1.0, 0.0).astype(BF16)
        for h in range(NP):
            kv = kv_refs[h][ks, :]
            keys = jnp.where(low, kv, ko_ref[ks, :])
            half = lax.dot_general(lhs_ref[h], keys, (((1,), (1,)), ((), ())), preferred_element_type=F32)
            half = half + (0.5 * rep_ref[h]) * same[...]
            weight = (half + half * jnp.tanh(half)).astype(BF16) * allowed[...]
            part = jnp.dot(weight, kv, preferred_element_type=F32)
            if c == 0 and start is None:
                acc[h] = part
            else:
                acc[h] = (acc if start is None or c else start)[h] + part


def early_kernel(tick, rep_ref, p_ref, pos_ref, bkt_ref, itm_ref, table_ref, qg_ref, kv_ref, cpos_ref, cbkt_ref, citm_ref, cown_ref, cother_ref, acc, qpos, qitm, lhs, ko, krow, same, allowed, cko):
    prepare(tick, p_ref, pos_ref, bkt_ref, itm_ref, table_ref, qg_ref, cbkt_ref, 0, qpos, qitm, lhs, ko, krow, cko)
    shared = (rep_ref, lhs, qpos, qitm, same, allowed, acc)
    add_keys(*shared, (kv_ref.at[0], kv_ref.at[1]), ko, krow.at[0:1], krow.at[1:2], None)
    add_keys(*shared, (cown_ref, cother_ref), cko, cpos_ref, citm_ref, acc)


def late_kernel(tick, rep_ref, p_ref, pos_ref, bkt_ref, itm_ref, table_ref, qg_ref, acc_ref, far_ref, out_ref, qpos, qitm, lhs, ko, krow, same, allowed, acc):
    prepare(tick, p_ref, pos_ref, bkt_ref, itm_ref, table_ref, qg_ref, None, 1, qpos, qitm, lhs, ko, krow, None)
    shared = (rep_ref, lhs, qpos, qitm, same, allowed, acc)
    add_keys(*shared, (far_ref.at[1], far_ref.at[0]), ko, krow.at[0:1], krow.at[1:2], acc_ref)
    low = low_lanes(BAND)
    out_ref[:, : 2 * DH] = (jnp.where(low, pltpu.roll(acc[0], DH, 1), acc[1]) * (1.0 / NK)).astype(BF16)
    gate = jnp.where(low, pltpu.roll(qg_ref[0].astype(F32), DH, 1), qg_ref[1].astype(F32))
    out_ref[:, 2 * DH :] = gate.astype(BF16)


SCRATCH = [
    pltpu.VMEM((BAND, 128), jnp.int32),
    pltpu.VMEM((BAND, 128), jnp.int32),
    pltpu.VMEM((NP, BAND, 2 * DH), BF16),
    pltpu.VMEM((BAND, 128), BF16),
    pltpu.VMEM((8, BAND), jnp.int32),
    pltpu.VMEM((BAND, KBLOCK), F32),
    pltpu.VMEM((BAND, KBLOCK), BF16),
]
ACC = pltpu.VMEM((NP, BAND, 2 * DH), F32)
CACHE_BUCKETS = pltpu.VMEM((CACHE, 128), BF16)


def attend(kernel, tick, shape, dtype, scratch, *operands):
    return pl.pallas_call(
        functools.partial(kernel, tick),
        out_shape=jax.ShapeDtypeStruct(shape, dtype),
        in_specs=[smem() if a.ndim == 1 else vmem() for a in operands],
        out_specs=vmem(),
        scratch_shapes=scratch,
        compiler_params=params(),
        name="attend_" + kernel.__name__,
    )(*operands)


def finish_rows(r_ref, x_ref, w_ref, gain_ref, mixed):
    total = jnp.zeros((ROWS, 2 * DH), F32)
    square = jnp.zeros((ROWS, 2 * DH), F32)
    for k in range(NG):
        a = r_ref[k, :, : 2 * DH].astype(F32)
        total += a
        square += a * a
    mean = jnp.sum(total, axis=-1, keepdims=True) * (1.0 / D)
    variance = jnp.sum(square, axis=-1, keepdims=True) * (1.0 / D) - mean * mean
    scale = lax.rsqrt(variance + EPSILON)
    for k in range(NG):
        cols = slice(k * 2 * DH, (k + 1) * 2 * DH)
        r = r_ref[k].astype(F32)
        mixed[:, cols] = ((r[:, : 2 * DH] - mean) * scale * gain_ref[:, cols] * r[:, 2 * DH :]).astype(BF16)
    y = jnp.dot(mixed[...], w_ref[...], preferred_element_type=F32)
    return (x_ref[...].astype(F32) + y).astype(BF16)


def finish_kernel(r_ref, x_ref, w_ref, gain_ref, out_ref, mixed):
    out_ref[...] = finish_rows(r_ref, x_ref, w_ref, gain_ref, mixed)


def last_kernel(before_ref, r_ref, x_ref, w_ref, gain_ref, out_ref, mixed):
    out_ref[0] = before_ref[...]
    out_ref[1] = finish_rows(r_ref, x_ref, w_ref, gain_ref, mixed)


def finish(*operands):
    last = len(operands) == 5
    return pl.pallas_call(
        last_kernel if last else finish_kernel,
        out_shape=jax.ShapeDtypeStruct((TICKS, ROWS, D) if last else (ROWS, D), BF16),
        in_specs=[vmem()] * len(operands),
        out_specs=vmem(),
        scratch_shapes=[pltpu.VMEM((ROWS, D), BF16)],
        compiler_params=params(),
        name="finish_last" if last else "finish",
    )(*operands)


def partner(i):
    return (i // NG ^ 1) * NG + (i % NG ^ NG // 2)


def swap(x):
    return lax.ppermute(x, ("p", "g"), [(i, partner(i)) for i in range(H)])


def body(
    slices,
    new_slice,
    w_qkv,
    w_gate,
    w_out,
    input_gain,
    output_gain,
    bucket_bias,
    repeat_bias,
    cache_kv,
    slice_positions,
    slice_buckets,
    slice_items,
    cache_positions,
    cache_buckets,
    cache_items,
):
    p = lax.axis_index("p")
    g = lax.axis_index("g")
    section = lax.axis_index("section")

    def pair(a):
        there = (1 - p) * NG + (g + NG // 2) % NG
        return jnp.concatenate([lax.dynamic_slice_in_dim(a, i, 1) for i in (p * NG + g, there)])

    gain_out = output_gain[0].reshape(NP, NG, DH)
    gain_out = jnp.where(p == 0, gain_out, gain_out[::-1])
    gain_out = jnp.stack([gain_out[0], jnp.roll(gain_out[1], NG // 2, 0)], axis=1).reshape(1, D)
    tables = pair(bucket_bias[0])
    rep = pair(repeat_bias[0])
    levels = jnp.arange(NB, dtype=jnp.int32)
    distance = jnp.abs(levels[:, None] - levels[None, :])
    lookup = (distance[:, :, None] == levels[None, None, :]).astype(F32)
    toeplitz = jnp.einsum("abc,hc->hab", lookup, tables.astype(F32)).astype(BF16)
    toeplitz = jnp.pad(0.5 * toeplitz, ((0, 0), (0, DH), (DH, 0)))
    p_word = p.astype(jnp.int32).reshape(1)
    received = slices[0]
    first = jnp.zeros((1,), jnp.int32)
    produced = ()
    for tick in range(TICKS):
        current, copies = spread(first, received, new_slice, input_gain)
        if tick == 0:
            copies, w_qkv, w_gate, w_out, cache_kv = lax.optimization_barrier((copies, w_qkv, w_gate, w_out, cache_kv))
            w_own = jnp.concatenate([w_qkv[0, :, :DH], w_gate[0], w_qkv[0, :, DH:]], axis=1)
            w_other = swap(w_own)
            c_own = cache_kv[0, :, 0, :]
            c_other = swap(c_own)
            w_pair = jnp.concatenate([w_out[0], swap(w_out[0])])
            w_copies = jnp.broadcast_to(w_pair[None], (NG, 2 * DH, D))
        band = lax.all_to_all(copies, "g", 0, 0)
        if tick == 0:
            band, w_own, w_other, c_other, rep, toeplitz, gain_out, w_copies = lax.optimization_barrier(
                (band, w_own, w_other, c_other, rep, toeplitz, gain_out, w_copies)
            )
        qg, kv, token = project(band, w_own, w_other)
        far = swap(kv)
        if tick == 0:
            w_copies, token = lax.optimization_barrier((w_copies, token))
            w_out_full = lax.all_to_all(w_copies, "g", 0, 0).reshape(D, D)
        keyed = (tick, (NP, BAND, 2 * DH), F32, SCRATCH + [CACHE_BUCKETS])
        given = (rep, p_word, slice_positions[0], slice_buckets[0], slice_items[0], toeplitz, qg)
        acc = attend(early_kernel, *keyed, *given, kv, cache_positions, cache_buckets, cache_items, c_own, c_other)
        a = attend(late_kernel, tick, (BAND, 4 * DH), BF16, SCRATCH + [ACC], *given, acc, far)
        if tick == 0:
            a, w_out_full = lax.optimization_barrier((a, w_out_full))
        back = lax.all_to_all(a.reshape(NG, ROWS, 4 * DH), "g", 0, 0)
        if tick + 1 < TICKS:
            one = finish(back, current, w_out_full, gain_out)
            produced = (one,)
            count = lax.axis_size("section")
            received = lax.ppermute(one, "section", [(s, s + 1) for s in range(count - 1)])
            first = (section == 0).astype(jnp.int32).reshape(1)
    return finish(*produced, back, current, w_out_full, gain_out)[None]


def solution(mesh):
    sections = mesh.shape["section"]
    grid = Mesh(mesh.devices.reshape(sections, NP, NG), ("section", "p", "g"))
    seq = ("p", "g")
    in_specs = (
        P("section", seq, None),
        P(seq, None),
        P("section", None, seq),
        P("section", None, seq),
        P("section", seq, None),
        P("section", None),
        P("section", None),
        P("section", None, None),
        P("section", None),
        P("section", None, seq, None),
        P("section", None, None),
        P("section", None, None),
        P("section", None, None),
        P("section", None),
        P("section", None),
        P("section", None),
    )
    out_specs = P("section", None, seq, None)
    return jax.shard_map(body, mesh=grid, in_specs=in_specs, out_specs=out_specs, check_vma=False)
```

```python
import functools

import jax
import jax.numpy as jnp
from jax import lax
from jax.experimental import pallas as pl
from jax.experimental.pallas import tpu as pltpu
from jax.sharding import Mesh, PartitionSpec as P

D = 1024
H = 16
DH = 64
NB = 64
TICKS = 2
CACHE = 768
SLICE = 2048
NK = CACHE + SLICE
EPSILON = 1e-05
NP = 2
NG = 8
ROWS = SLICE // (NP * NG)
BAND = SLICE // NP
KBLOCK = 256
BF16 = jnp.bfloat16
F32 = jnp.float32
VMEM_LIMIT = 24 * 1024 * 1024


def silu(v):
    half = 0.5 * v
    return half + half * jnp.tanh(half)


def vmem():
    return pl.BlockSpec(memory_space=pltpu.VMEM)


def smem():
    return pl.BlockSpec(memory_space=pltpu.SMEM)


def params():
    return pltpu.CompilerParams(vmem_limit_bytes=VMEM_LIMIT)


def low_lanes(rows):
    return lax.broadcasted_iota(jnp.int32, (rows, 2 * DH), 1) < DH


def spread_kernel(first_ref, x_ref, new_ref, gain_ref, here_ref, out_ref):
    fresh = jnp.full((ROWS, 1), first_ref[0], jnp.int32) > 0
    here = jnp.where(fresh, new_ref[...].astype(F32), x_ref[...].astype(F32))
    here_ref[...] = here.astype(BF16)
    mean = jnp.mean(here, axis=-1, keepdims=True)
    variance = jnp.mean(here * here, axis=-1, keepdims=True) - mean * mean
    normed = ((here - mean) * lax.rsqrt(variance + EPSILON) * gain_ref[...]).astype(BF16)
    for k in range(NG):
        out_ref[k] = normed


def spread(*operands):
    return pl.pallas_call(
        spread_kernel,
        out_shape=(jax.ShapeDtypeStruct((ROWS, D), BF16), jax.ShapeDtypeStruct((NG, ROWS, D), BF16)),
        in_specs=[smem()] + [vmem()] * 3,
        out_specs=(vmem(),) * 2,
        compiler_params=params(),
        name="spread",
    )(*operands)


def open_kernel(x_ref, gain_ref, out_ref):
    here = x_ref[...].astype(F32)
    mean = jnp.mean(here, axis=-1, keepdims=True)
    variance = jnp.mean(here * here, axis=-1, keepdims=True) - mean * mean
    normed = ((here - mean) * lax.rsqrt(variance + EPSILON) * gain_ref[...]).astype(BF16)
    for k in range(NG):
        out_ref[k] = normed


def copies_kernel(own_ref, other_ref, out_ref):
    for k in range(NG):
        out_ref[k, :DH, :] = own_ref[...]
        out_ref[k, DH:, :] = other_ref[...]


def copies_of(kernel, *operands):
    return pl.pallas_call(
        kernel,
        out_shape=jax.ShapeDtypeStruct((NG, ROWS, D), BF16),
        in_specs=[vmem()] * 2,
        out_specs=vmem(),
        compiler_params=params(),
        name=kernel.__name__,
    )(*operands)


def column(row):
    return jnp.transpose(jnp.broadcast_to(row, (128, row.shape[1])))


def prepare(tick, p_ref, pos_ref, bkt_ref, itm_ref, table_ref, qg_ref, cbkt_ref, far, qpos, qitm, lhs, ko, krow, cko):
    lane = lax.broadcasted_iota(jnp.int32, (BAND, 128), 1)
    flip = jnp.full((1, BAND), p_ref[0], jnp.int32) > 0

    def bands(ref):
        low, high = ref[tick : tick + 1, :BAND], ref[tick : tick + 1, BAND:]
        return jnp.where(flip, high, low), jnp.where(flip, low, high)

    pos, bkt, itm = bands(pos_ref), bands(bkt_ref), bands(itm_ref)
    qpos[...] = column(pos[0])
    qitm[...] = column(itm[0])
    krow[0:1, :] = pos[far]
    krow[1:2, :] = itm[far]
    level = column(bkt[0])
    onehot = jnp.where(level == lane, 1.0, 0.0).astype(BF16)
    for h in range(NP):
        bias = jnp.dot(onehot, table_ref[h], preferred_element_type=F32)
        lhs[h] = jnp.where(lane < DH, qg_ref[h].astype(F32), bias).astype(BF16)
    level = column(bkt[1]) if far else level
    ko[...] = jnp.where(level == lane - DH, 1.0, 0.0).astype(BF16)
    if not far:
        cko[...] = jnp.where(column(cbkt_ref[...]) == lane[:CACHE] - DH, 1.0, 0.0).astype(BF16)


def project_kernel(x_ref, own_ref, other_ref, *refs):
    qg_ref, kv_ref = refs[-2:]
    normed = x_ref[...].reshape(BAND, D)
    scale = jnp.where(low_lanes(BAND), 0.5, 1.0)
    for h, w_ref in enumerate((own_ref, other_ref)):
        z = silu(jnp.dot(normed, w_ref[...], preferred_element_type=F32))
        kv_ref[h] = z[:, 2 * DH :].astype(BF16)
        qg_ref[h] = (z[:, : 2 * DH] * scale).astype(BF16)


def project(*operands):
    return pl.pallas_call(
        project_kernel,
        out_shape=(
            jax.ShapeDtypeStruct((NP, BAND, 2 * DH), BF16),
            jax.ShapeDtypeStruct((NP, BAND, 2 * DH), BF16),
        ),
        in_specs=[vmem()] * 3 + [pl.BlockSpec(memory_space=pl.ANY)] * (len(operands) - 3),
        out_specs=(vmem(),) * 2,
        compiler_params=params(),
        name="project",
    )(*operands)


def add_keys(rep_ref, lhs_ref, qpos_ref, qitm_ref, same, allowed, acc, kv_refs, ko_ref, kpos_ref, kitm_ref, start):
    low = low_lanes(KBLOCK)
    for c in range(kv_refs[0].shape[0] // KBLOCK):
        ks = slice(c * KBLOCK, (c + 1) * KBLOCK)
        wide = jnp.concatenate([qitm_ref[...]] * (KBLOCK // 128), axis=1)
        same[...] = jnp.where(wide == kitm_ref[:, ks], 1.0, 0.0)
        wide = jnp.concatenate([qpos_ref[...]] * (KBLOCK // 128), axis=1)
        allowed[...] = jnp.where(kpos_ref[:, ks] <= wide, 1.0, 0.0).astype(BF16)
        for h in range(NP):
            kv = kv_refs[h][ks, :]
            keys = jnp.where(low, kv, ko_ref[ks, :])
            half = lax.dot_general(lhs_ref[h], keys, (((1,), (1,)), ((), ())), preferred_element_type=F32)
            half = half + (0.5 * rep_ref[h]) * same[...]
            weight = (half + half * jnp.tanh(half)).astype(BF16) * allowed[...]
            part = jnp.dot(weight, kv, preferred_element_type=F32)
            if c == 0 and start is None:
                acc[h] = part
            else:
                acc[h] = (acc if start is None or c else start)[h] + part


def early_kernel(tick, rep_ref, p_ref, pos_ref, bkt_ref, itm_ref, table_ref, qg_ref, kv_ref, cpos_ref, cbkt_ref, citm_ref, cown_ref, cother_ref, acc, qpos, qitm, lhs, ko, krow, same, allowed, cko):
    prepare(tick, p_ref, pos_ref, bkt_ref, itm_ref, table_ref, qg_ref, cbkt_ref, 0, qpos, qitm, lhs, ko, krow, cko)
    shared = (rep_ref, lhs, qpos, qitm, same, allowed, acc)
    add_keys(*shared, (kv_ref.at[0], kv_ref.at[1]), ko, krow.at[0:1], krow.at[1:2], None)
    add_keys(*shared, (cown_ref, cother_ref), cko, cpos_ref, citm_ref, acc)


def late_kernel(tick, rep_ref, p_ref, pos_ref, bkt_ref, itm_ref, table_ref, qg_ref, acc_ref, far_ref, out_ref, qpos, qitm, lhs, ko, krow, same, allowed, acc):
    prepare(tick, p_ref, pos_ref, bkt_ref, itm_ref, table_ref, qg_ref, None, 1, qpos, qitm, lhs, ko, krow, None)
    shared = (rep_ref, lhs, qpos, qitm, same, allowed, acc)
    add_keys(*shared, (far_ref.at[1], far_ref.at[0]), ko, krow.at[0:1], krow.at[1:2], acc_ref)
    low = low_lanes(BAND)
    out_ref[:, : 2 * DH] = (jnp.where(low, pltpu.roll(acc[0], DH, 1), acc[1]) * (1.0 / NK)).astype(BF16)
    gate = jnp.where(low, pltpu.roll(qg_ref[0].astype(F32), DH, 1), qg_ref[1].astype(F32))
    out_ref[:, 2 * DH :] = gate.astype(BF16)


SCRATCH = [
    pltpu.VMEM((BAND, 128), jnp.int32),
    pltpu.VMEM((BAND, 128), jnp.int32),
    pltpu.VMEM((NP, BAND, 2 * DH), BF16),
    pltpu.VMEM((BAND, 128), BF16),
    pltpu.VMEM((8, BAND), jnp.int32),
    pltpu.VMEM((BAND, KBLOCK), F32),
    pltpu.VMEM((BAND, KBLOCK), BF16),
]
ACC = pltpu.VMEM((NP, BAND, 2 * DH), F32)
CACHE_BUCKETS = pltpu.VMEM((CACHE, 128), BF16)


def attend(kernel, tick, shape, dtype, scratch, *operands):
    return pl.pallas_call(
        functools.partial(kernel, tick),
        out_shape=jax.ShapeDtypeStruct(shape, dtype),
        in_specs=[smem() if a.ndim == 1 else vmem() for a in operands],
        out_specs=vmem(),
        scratch_shapes=scratch,
        compiler_params=params(),
        name="attend_" + kernel.__name__,
    )(*operands)


def finish_rows(r_ref, x_ref, w_ref, gain_ref, mixed):
    total = jnp.zeros((ROWS, 2 * DH), F32)
    square = jnp.zeros((ROWS, 2 * DH), F32)
    for k in range(NG):
        a = r_ref[k, :, : 2 * DH].astype(F32)
        total += a
        square += a * a
    mean = jnp.sum(total, axis=-1, keepdims=True) * (1.0 / D)
    variance = jnp.sum(square, axis=-1, keepdims=True) * (1.0 / D) - mean * mean
    scale = lax.rsqrt(variance + EPSILON)
    for k in range(NG):
        cols = slice(k * 2 * DH, (k + 1) * 2 * DH)
        r = r_ref[k].astype(F32)
        mixed[:, cols] = ((r[:, : 2 * DH] - mean) * scale * gain_ref[:, cols] * r[:, 2 * DH :]).astype(BF16)
    y = jnp.dot(mixed[...], w_ref[...], preferred_element_type=F32)
    return (x_ref[...].astype(F32) + y).astype(BF16)


def finish_kernel(r_ref, x_ref, w_ref, gain_ref, out_ref, mixed):
    out_ref[...] = finish_rows(r_ref, x_ref, w_ref, gain_ref, mixed)


def last_kernel(before_ref, r_ref, x_ref, w_ref, gain_ref, out_ref, mixed):
    out_ref[0] = before_ref[...]
    out_ref[1] = finish_rows(r_ref, x_ref, w_ref, gain_ref, mixed)


def finish(*operands):
    last = len(operands) == 5
    return pl.pallas_call(
        last_kernel if last else finish_kernel,
        out_shape=jax.ShapeDtypeStruct((TICKS, ROWS, D) if last else (ROWS, D), BF16),
        in_specs=[vmem()] * len(operands),
        out_specs=vmem(),
        scratch_shapes=[pltpu.VMEM((ROWS, D), BF16)],
        compiler_params=params(),
        name="finish_last" if last else "finish",
    )(*operands)


def partner(i):
    return (i // NG ^ 1) * NG + (i % NG ^ NG // 2)


def swap(x):
    return lax.ppermute(x, ("p", "g"), [(i, partner(i)) for i in range(H)])


def body(
    slices,
    new_slice,
    w_qkv,
    w_gate,
    w_out,
    input_gain,
    output_gain,
    bucket_bias,
    repeat_bias,
    cache_kv,
    slice_positions,
    slice_buckets,
    slice_items,
    cache_positions,
    cache_buckets,
    cache_items,
):
    p = lax.axis_index("p")
    g = lax.axis_index("g")
    section = lax.axis_index("section")

    def pair(a):
        there = (1 - p) * NG + (g + NG // 2) % NG
        return jnp.concatenate([lax.dynamic_slice_in_dim(a, i, 1) for i in (p * NG + g, there)])

    gain_out = output_gain[0].reshape(NP, NG, DH)
    gain_out = jnp.where(p == 0, gain_out, gain_out[::-1])
    gain_out = jnp.stack([gain_out[0], jnp.roll(gain_out[1], NG // 2, 0)], axis=1).reshape(1, D)
    tables = pair(bucket_bias[0])
    rep = pair(repeat_bias[0])
    levels = jnp.arange(NB, dtype=jnp.int32)
    distance = jnp.abs(levels[:, None] - levels[None, :])
    lookup = (distance[:, :, None] == levels[None, None, :]).astype(F32)
    toeplitz = jnp.einsum("abc,hc->hab", lookup, tables.astype(F32)).astype(BF16)
    toeplitz = jnp.pad(0.5 * toeplitz, ((0, 0), (0, DH), (DH, 0)))
    p_word = p.astype(jnp.int32).reshape(1)
    received = slices[0]
    first = jnp.zeros((1,), jnp.int32)
    produced = ()
    for tick in range(TICKS):
        if tick == 0:
            current, copies = received, copies_of(open_kernel, received, input_gain)
        else:
            current, copies = spread(first, received, new_slice, input_gain)
        if tick == 0:
            copies, w_qkv, w_gate, w_out, cache_kv = lax.optimization_barrier((copies, w_qkv, w_gate, w_out, cache_kv))
            w_own = jnp.concatenate([w_qkv[0, :, :DH], w_gate[0], w_qkv[0, :, DH:]], axis=1)
            w_other = swap(w_own)
            c_own = cache_kv[0, :, 0, :]
            c_other = swap(c_own)
            w_copies = copies_of(copies_kernel, w_out[0], swap(w_out[0]))
        band = lax.all_to_all(copies, "g", 0, 0)
        if tick == 0:
            token = band[0, :16, :128]
            token, w_own, w_other, c_other, rep, toeplitz, gain_out, w_copies = lax.optimization_barrier(
                (token, w_own, w_other, c_other, rep, toeplitz, gain_out, w_copies)
            )
            w_out_full = lax.all_to_all(w_copies, "g", 0, 0).reshape(D, D)
            qg, kv = project(band, w_own, w_other, token)
        else:
            qg, kv = project(band, w_own, w_other)
        far = swap(kv)
        keyed = (tick, (NP, BAND, 2 * DH), F32, SCRATCH + [CACHE_BUCKETS])
        given = (rep, p_word, slice_positions[0], slice_buckets[0], slice_items[0], toeplitz, qg)
        acc = attend(early_kernel, *keyed, *given, kv, cache_positions, cache_buckets, cache_items, c_own, c_other)
        a = attend(late_kernel, tick, (BAND, 4 * DH), BF16, SCRATCH + [ACC], *given, acc, far)
        if tick == 0:
            a, w_out_full = lax.optimization_barrier((a, w_out_full))
        back = lax.all_to_all(a.reshape(NG, ROWS, 4 * DH), "g", 0, 0)
        if tick + 1 < TICKS:
            one = finish(back, current, w_out_full, gain_out)
            produced = (one,)
            count = lax.axis_size("section")
            received = lax.ppermute(one, "section", [(s, s + 1) for s in range(count - 1)])
            first = (section == 0).astype(jnp.int32).reshape(1)
    return finish(*produced, back, current, w_out_full, gain_out)[None]


def solution(mesh):
    sections = mesh.shape["section"]
    grid = Mesh(mesh.devices.reshape(sections, NP, NG), ("section", "p", "g"))
    seq = ("p", "g")
    in_specs = (
        P("section", seq, None),
        P(seq, None),
        P("section", None, seq),
        P("section", None, seq),
        P("section", seq, None),
        P("section", None),
        P("section", None),
        P("section", None, None),
        P("section", None),
        P("section", None, seq, None),
        P("section", None, None),
        P("section", None, None),
        P("section", None, None),
        P("section", None),
        P("section", None),
        P("section", None),
    )
    out_specs = P("section", None, seq, None)
    return jax.shard_map(body, mesh=grid, in_specs=in_specs, out_specs=out_specs, check_vma=False)
```
